512 devices in a mesh: section: 8 (over y), dp: 4 (over x_lo, core), tensor: 16 (over x_hi, z).
Axes of the slice: x: 4 (x_hi: 2, x_lo: 2; x = x_hi * 2 + x_lo), y: 8, z: 8, core: 2. Of those that a mesh axis runs over, the one named last changes fastest.
Arguments:
- train_act: bfloat16 [8, 4096, 5120], P('section', ('dp', 'tensor')), may hold values from -0.75 to 0.75
- train_grad: bfloat16 [8, 4096, 27648], P('section', 'dp', 'tensor'), may hold values from -0.5 to 0.5
- val_act: bfloat16 [8, 512, 5120], P('section', ('dp', 'tensor')), may hold values from -0.75 to 0.75
- val_grad: bfloat16 [8, 512, 27648], P('section', 'dp', 'tensor'), may hold values from -0.5 to 0.5
- segment_ids: int32 [4, 1024], P('dp'), may hold values from 0 to 3, never falling along the last dimension, each value on 1 to 512 neighbouring positions
- val_lengths: int32 [8], replicated, may hold values from 1 to 64, 384 in all
Outputs:
- scores: float32 [4, 4], P('dp')
The draws below stay inside these ranges and needn't reach their ends.
Inputs may be any that keep to these rules, and one draw needn't show every extreme that they name: `segment_ids`: ids never fall along a row, each of the 4 ids holds 1 to 512 tokens of every row, and one holds exactly that many. `val_lengths`: the lengths sum to 384 and the largest is exactly 64.
All inputs are finite; a program needn't handle non-finite values.
Results may differ from the reference program's by a relative error of at most 0.0003.
Values may be sent and summed in bfloat16 or wider, within the bound.
No kernel may reach another device: no remote copies, remote signals or barrier semaphores. Data moves between devices by JAX's collectives and lax.ppermute only.
A program may use at most 64 MiB of HBM per device.

```python
import math
import jax
import jax.numpy as jnp
import numpy as np
from jax import lax

D = 5120
FF = 27648
TOK_DEV = 1024
SEQ_DEV = 4
VSEQ = 8
VLEN = 64
SECTIONS = 8
TOKENS = 4096
VTOK = 512
N_SECTION = 8
N_DP = 4


def block_scale(rng, extent, pieces, smallest, top_value):
    gain = 1.0
    for position, shards_of in pieces:
        draws = jax.random.uniform(jax.random.fold_in(jax.random.fold_in(rng, 6), position), (shards_of,), jnp.float32, smallest / len(pieces), top_value / len(pieces))
        gain = gain * jnp.repeat(jnp.exp(draws), extent[position] // shards_of).reshape((-1,) + (1,) * (len(extent) - 1 - position))
    return gain


def split_up(count, total, limit, lean):
    loads = [(1 << 20) // math.isqrt(grade ** lean) + 1 for grade in range(2, count + 1)]
    spare, given = total - limit - (count - 1), [1] * (count - 1)
    while spare > 0:
        movable = [i for i in range(count - 1) if given[i] < limit]
        pool, remaining = sum([loads[i] for i in movable]), spare
        for i in movable:
            more = min(limit - given[i], max(1, remaining * loads[i] // pool), spare)
            given[i] = given[i] + more
            spare = spare - more
    return np.array([limit] + given)


def uneven_parts(key, count, total, limit, lean):
    if count == 2:
        one = jax.random.randint(key, (), max(1, total - limit), min(limit, total - 1) + 1)
        return jnp.stack([one, total - one])
    sizes = jnp.asarray(split_up(count, total, limit, lean), jnp.int32)
    couples = (count - 1) // 2
    donor, taker = sizes[1:1 + 2 * couples:2], sizes[2:2 + 2 * couples:2]
    room = jnp.minimum(donor - 1, limit - taker)
    moved = jax.random.randint(jax.random.fold_in(key, 1), (couples,), 0, 1 << 20) % (room + 1)
    sizes = sizes.at[1:1 + 2 * couples:2].set(donor - moved).at[2:2 + 2 * couples:2].set(taker + moved)
    return sizes[jax.random.permutation(jax.random.fold_in(key, 2), count)]


def gaussian(own_key, extent, scale, most, cuts=(), kind=jnp.bfloat16):
    drawn = jax.random.normal(own_key, extent, jnp.float32) * scale
    if len(cuts) > 0:
        drawn = block_scale(own_key, extent, cuts, -0.22, 0.18) * drawn
    return jnp.clip(drawn, min=-most, max=most).astype(kind)


def setup_inputs(seed: int = 0) -> dict:
    keys = jax.random.split(jax.random.key(seed), 7)
    train_act = gaussian(keys[0], (SECTIONS, TOKENS, D), (D ** -0.25), 0.75, ((0, 8), (1, 64)))
    train_grad = gaussian(keys[1], (SECTIONS, TOKENS, FF), (FF ** -0.25), 0.5, ((0, 8), (1, 4), (2, 16)))
    val_act = gaussian(keys[2], (SECTIONS, VTOK, D), (D ** -0.25), 0.75, ((0, 8), (1, 64)))
    val_grad = gaussian(keys[3], (SECTIONS, VTOK, FF), (FF ** -0.25), 0.5, ((0, 8), (1, 4), (2, 16)))
    segment_ids = jax.vmap(lambda own: jnp.searchsorted(jnp.cumsum(uneven_parts(own, SEQ_DEV, TOK_DEV, TOK_DEV // 2, 2)), jnp.arange(TOK_DEV), side="right"))(jax.random.split(keys[4], N_DP)).reshape((N_DP, TOK_DEV)).astype(jnp.int32)
    val_lengths = uneven_parts(keys[5], VSEQ, 6 * VLEN, VLEN, 2).astype(jnp.int32)
    return {"train_act": train_act, "train_grad": train_grad, "val_act": val_act, "val_grad": val_grad, "segment_ids": segment_ids, "val_lengths": val_lengths}


def reference(train_act, train_grad, val_act, val_grad, segment_ids, val_lengths):
    positions = jnp.arange(VLEN, dtype=jnp.int32)
    live = (positions[None, :] < val_lengths[:, None]).astype(jnp.float32).reshape(VSEQ * VLEN)

    def one_section(items):
        act_rows, grad_rows, val_act_rows, val_grad_rows = items
        act_gram = jnp.dot(act_rows, val_act_rows.T, preferred_element_type=jnp.float32)
        grad_gram = jnp.dot(grad_rows, val_grad_rows.T, preferred_element_type=jnp.float32)
        return jnp.dot(act_gram * grad_gram, live, precision=lax.Precision.HIGHEST)
    per_token = lax.map(one_section, (train_act, train_grad, val_act, val_grad))
    summed = lax.optimization_barrier(jnp.sum(per_token, axis=0)).reshape(N_DP, TOK_DEV)
    onehot = (segment_ids[:, None, :] == jnp.arange(SEQ_DEV, dtype=jnp.int32)[None, :, None]).astype(jnp.float32)
    scores = lax.optimization_barrier(jnp.sum(onehot * summed[:, None, :], axis=2))
    return scores / jnp.sqrt(jnp.float32(TOK_DEV * VSEQ * VLEN * N_SECTION))
```

```python
import jax
import jax.numpy as jnp
from jax import lax
from jax.sharding import Mesh, PartitionSpec as P

SEQ_DEV = 4
VSEQ = 8
VLEN = 64
VLIVE = 384

NAMES = ("section", "pair", "core", "far", "depth")
SHAPE = (8, 2, 2, 2, 8)
PLANE = ("pair", "core", "far", "depth")
SLICES = ("pair", "core", "far")
TENSOR = ("far", "depth")
LAYERS = ("section", "far", "depth")


def swap(value, axis):
    return lax.ppermute(value, axis, [(0, 1), (1, 0)])


def trade(value, axes):
    return lax.all_to_all(value, axes, 0, 0, tiled=True)


def rows_gram(left, right):
    dims = (((1,), (1,)), ((), ()))
    return lax.dot_general(left, right, dims, preferred_element_type=jnp.float32)


def on_device(train_act, train_grad, val_act, val_grad, segment_ids, val_lengths):
    tok_count = segment_ids.shape[1]
    rows, width = train_act.shape[1:]
    val_rows = val_act.shape[1]
    parts = lax.axis_size(SLICES)
    planes = lax.axis_size(PLANE)
    depth = lax.axis_size("depth")
    sharers = lax.axis_size(TENSOR)
    piece = width // parts
    slots = VSEQ * VLEN

    positions = jnp.arange(VLEN, dtype=jnp.int32)
    starts = jnp.cumsum(val_lengths) - val_lengths
    rank = jnp.where(positions[None, :] < val_lengths[:, None], starts[:, None] + positions[None, :], -1)
    live_index = jnp.arange(VLIVE, dtype=jnp.int32)
    pick = (rank.reshape(1, slots) == live_index[:, None]).astype(jnp.bfloat16)

    own = val_grad[0]
    across = swap(own, "pair")
    beside = swap(own, "core")
    corner = swap(across, "core")

    acts = val_act[0].reshape(val_rows, parts, piece).transpose(1, 0, 2)
    acts = jnp.broadcast_to(acts[:, None], (parts, depth, val_rows, piece))
    val_acts = trade(acts.reshape(planes, val_rows, piece), PLANE).reshape(slots, piece)
    train_acts = trade(train_act[0].reshape(rows, parts, piece).transpose(1, 0, 2), SLICES)

    here = lax.axis_index("pair") * 2 + lax.axis_index("core")
    order = jnp.stack([here, here ^ 1, here ^ 2, here ^ 3])
    ranks = rank.reshape(4, slots // 4)[order].reshape(1, slots)
    pick_grad = (ranks == live_index[:, None]).astype(jnp.bfloat16)
    val_grads = jnp.concatenate([own, beside, across, corner], axis=0)
    live_grads = jnp.dot(pick_grad, val_grads, preferred_element_type=jnp.float32).astype(jnp.bfloat16)
    grad_part = rows_gram(train_grad[0], live_grads)
    grad_gram = jnp.sum(trade(grad_part.reshape(sharers, rows, VLIVE), TENSOR), axis=0)

    live_acts = jnp.dot(pick, val_acts, preferred_element_type=jnp.float32).astype(jnp.bfloat16)
    act_part = rows_gram(train_acts.reshape(parts * rows, piece), live_acts)
    act_gram = jnp.sum(trade(act_part.reshape(parts, rows, VLIVE), SLICES), axis=0)

    per_token = jnp.sum(act_gram * grad_gram, axis=1)
    first = lax.axis_index(TENSOR) * rows
    ids = lax.dynamic_slice(segment_ids[0], (first,), (rows,))
    seq_numbers = jnp.arange(SEQ_DEV, dtype=jnp.int32)[:, None]
    terms = jnp.sum(jnp.where(ids[None, :] == seq_numbers, per_token[None, :], 0.0), axis=1)
    everyone = lax.axis_size(LAYERS)
    totals = jnp.sum(trade(jnp.broadcast_to(terms, (everyone, 1, SEQ_DEV)), LAYERS), axis=0)
    norm_factor = jnp.sqrt(jnp.float32(tok_count * slots * lax.axis_size("section")))
    return totals / norm_factor


def solution(mesh):
    split = Mesh(mesh.devices.reshape(SHAPE), NAMES)
    placed = (
        P("section", PLANE, None),
        P("section", ("pair", "core"), TENSOR),
        P("section", PLANE, None),
        P("section", ("pair", "core"), TENSOR),
        P(("pair", "core"), None),
        P(),
    )
    return jax.shard_map(
        on_device, mesh=split, in_specs=placed, out_specs=P(("pair", "core"), None), check_vma=False
    )
```

```python
import functools
import jax
import jax.numpy as jnp
from jax import lax
from jax.experimental import pallas as pl
from jax.experimental.pallas import tpu as pltpu
from jax.sharding import Mesh, PartitionSpec as P

SEQ_DEV = 4
VSEQ = 8
VLEN = 64
SLOTS = VSEQ * VLEN
LIVE = 384
TILE = 512

NAMES = ("section", "pair", "core", "far", "depth")
SHAPE = (8, 2, 2, 2, 8)
PLANE = ("pair", "core", "far", "depth")
SLICES = ("core", "pair", "far")
ACROSS = ("core", "pair", "far", "depth")
TENSOR = ("far", "depth")
LAYERS = ("section", "far", "depth")

SMEM = pl.BlockSpec(memory_space=pltpu.SMEM)
VMEM = pl.BlockSpec(memory_space=pltpu.VMEM)
LIMIT = 48 * 1024 * 1024


def swap(value, axis):
    return lax.ppermute(value, axis, [(0, 1), (1, 0)])


def trade(value, axes):
    return lax.all_to_all(value, axes, 0, 0, tiled=True)


def dot(left, right, over):
    return lax.dot_general(left, right, (over, ((), ())), preferred_element_type=jnp.float32)


def params(**more):
    return pltpu.CompilerParams(vmem_limit_bytes=LIMIT, **more)


def cost(flops, moved):
    return pl.CostEstimate(flops=flops, bytes_accessed=moved, transcendentals=0)


def live_places(lens, seq, pos):
    place = jnp.full(seq.shape, -1, jnp.int32)
    start = jnp.int32(0)
    for number in range(VSEQ):
        count = lens[number]
        place = jnp.where((seq == number) & (pos < count), start + pos, place)
        start = start + count
    return place


def picker(place):
    wanted = lax.broadcasted_iota(jnp.int32, (LIVE, place.shape[1]), 0)
    return jnp.where(wanted == place, 1.0, 0.0).astype(jnp.bfloat16)


def live_part(spot, lens, pieces, first):
    here = spot[0] * 2 + spot[1]
    lane = lax.broadcasted_iota(jnp.int32, (1, SLOTS // 2), 1)
    quarter = SLOTS // 4
    owner = jnp.where(lane < quarter, here ^ first, here ^ (first + 1))
    within = lane % quarter
    place = live_places(lens, owner * 2 + within // VLEN, within % VLEN)
    both = jnp.concatenate([pieces[0][...], pieces[1][...]], axis=1)
    return dot(picker(place), both, ((1,), (1,))).astype(jnp.bfloat16)


def near_kernel(spot, lens, own, beside, near):
    near[...] = live_part(spot, lens, (own, beside), 0)


def near_call(spot, lens, own, beside):
    feats = own.shape[0]
    return pl.pallas_call(
        near_kernel,
        out_shape=jax.ShapeDtypeStruct((LIVE, feats), jnp.bfloat16),
        in_specs=[SMEM, SMEM, VMEM, VMEM],
        out_specs=VMEM,
        compiler_params=params(),
        cost_estimate=cost(SLOTS * LIVE * feats, SLOTS * feats + 2 * LIVE * feats),
    )(spot, lens, own, beside)


def grad_kernel(spot, lens, near, across, corner, train, out, live):
    @pl.when(pl.program_id(0) == 0)
    def _():
        live[...] = near[...] + live_part(spot, lens, (across, corner), 2)

    out[...] = dot(live[...], train[...], ((1,), (0,))).T.reshape(out.shape)


def grad_call(spot, lens, near, across, corner, train, rows):
    feats, toks = train.shape
    depth = toks // (2 * rows)
    step = TILE // rows
    half = depth // step
    quarter = pl.BlockSpec((feats, SLOTS // 4), lambda i, spot, lens: (0, 0))
    return pl.pallas_call(
        grad_kernel,
        out_shape=jax.ShapeDtypeStruct((depth, 2, rows, LIVE), jnp.float32),
        grid_spec=pltpu.PrefetchScalarGridSpec(
            num_scalar_prefetch=2,
            grid=(toks // TILE,),
            in_specs=[
                pl.BlockSpec((LIVE, feats), lambda i, spot, lens: (0, 0)),
                quarter,
                quarter,
                pl.BlockSpec((feats, TILE), lambda i, spot, lens: (0, i)),
            ],
            out_specs=pl.BlockSpec((step, 1, rows, LIVE), lambda i, spot, lens: (i % half, i // half, 0, 0)),
            scratch_shapes=[pltpu.VMEM((LIVE, feats), jnp.bfloat16)],
        ),
        compiler_params=params(),
        cost_estimate=cost(2 * toks * LIVE * feats, 2 * toks * feats + 4 * toks * LIVE),
    )(spot, lens, near, across, corner, train)


def act_kernel(lens, mine, came, vals, away, keep):
    slots = vals.shape[0]
    lane = lax.broadcasted_iota(jnp.int32, (1, slots), 1)
    block = lane // VLEN
    seq = (block // 2 % 2) * 4 + (block // 4) * 2 + block % 2
    chosen = picker(live_places(lens, seq, lane % VLEN))
    live = dot(chosen, vals[...], ((1,), (0,))).astype(jnp.bfloat16)
    for flip, ref in enumerate((keep, away)):
        left = jnp.concatenate([part[pair, flip] for part in (mine, came) for pair in range(2)], axis=0)
        ref[...] = dot(left, live, ((1,), (1,))).reshape(ref.shape)


def act_call(lens, mine, came, vals):
    rows, piece = mine.shape[2:]
    shape = jax.ShapeDtypeStruct((2, 2, rows, LIVE), jnp.float32)
    count = 8 * rows
    return pl.pallas_call(
        act_kernel,
        out_shape=(shape, shape),
        in_specs=[SMEM, VMEM, VMEM, VMEM],
        out_specs=(VMEM, VMEM),
        compiler_params=params(),
        cost_estimate=cost(2 * (count + SLOTS) * LIVE * piece, 4 * SLOTS * piece + 4 * count * LIVE),
    )(lens, mine, came, vals)


def combine_kernel(spot, ids, act_a, act_b, grads, out):
    depth, _, rows, _ = grads.shape
    per = 128 // rows
    lane = lax.broadcasted_iota(jnp.int32, (8, 128), 1)
    seqs = lax.broadcasted_iota(jnp.int32, (8, rows), 0)
    total = jnp.zeros((8, LIVE), jnp.float32)
    for far in range(2):
        number = far * depth + spot[3]
        lanes = ids[:, pl.ds(pl.multiple_of((number // per) * 128, 128), 128)]
        owner = lanes[:, :rows]
        for turn in range(1, per):
            owner = jnp.where(number % per == turn, lanes[:, turn * rows : (turn + 1) * rows], owner)
        grad = grads[0, far]
        for other in range(1, depth):
            grad = grad + grads[other, far]
        flip = spot[2] ^ far
        terms = (act_a[flip] + act_b[1 - flip]) * grad
        total = total + lax.dot_general(
            jnp.where(seqs == owner, 1.0, 0.0), terms, (((1,), (0,)), ((), ())),
            precision=lax.Precision.HIGHEST, preferred_element_type=jnp.float32,
        )
    column = jnp.sum(total, axis=1, keepdims=True)
    square = lax.broadcasted_iota(jnp.int32, (8, 128), 0) == lane
    out[...] = jnp.sum(jnp.where(square, column, 0.0), axis=0, keepdims=True)


def combine_call(spot, ids, act_a, act_b, grads):
    return pl.pallas_call(
        combine_kernel,
        out_shape=jax.ShapeDtypeStruct((1, 128), jnp.float32),
        in_specs=[SMEM, VMEM, VMEM, VMEM, VMEM],
        out_specs=VMEM,
        compiler_params=params(),
        cost_estimate=cost(2 * grads.size, 4 * grads.size),
    )(spot, ids, act_a, act_b, grads)


def total_kernel(scale, terms, out):
    out[...] = jnp.sum(terms[...], axis=0, keepdims=True)[:, :SEQ_DEV] * scale


def on_device(train_act, train_grad, val_act, val_grad, segment_ids, val_lengths):
    tok_count = segment_ids.shape[1]
    rows, width = train_act.shape[1:]
    val_rows = val_act.shape[1]
    parts = lax.axis_size(SLICES)
    depth = lax.axis_size("depth")
    piece = width // parts
    pair, core, far, deep = (lax.axis_index(name) for name in PLANE)
    spot = jnp.stack([pair, core, far, deep]).astype(jnp.int32)

    own = val_grad[0].T
    across = swap(own, "pair")
    beside = swap(own, "core")
    corner = swap(across, "core")

    acts = val_act[0].reshape(val_rows, parts, piece).transpose(1, 0, 2)
    acts = jnp.broadcast_to(acts[:, None], (parts, depth, val_rows, piece))
    vals = trade(acts.reshape(parts * depth, val_rows, piece), ACROSS).reshape(SLOTS, piece)

    def step(value, index):
        left, right = jnp.split(value, 2, axis=-1)
        return jnp.where(index == 0, left, right), jnp.where(index == 0, right, left)

    kept, sent = step(train_act[0], core)
    came = swap(sent, "core")
    own_late, came = lax.optimization_barrier((own, came))
    near = near_call(spot, val_lengths, own_late, beside)
    kept, sent = step(jnp.stack([kept, came]), pair)
    sent, across = lax.optimization_barrier((sent, across))
    came = swap(sent, "pair")

    grad_part = grad_call(spot, val_lengths, near, across, corner, train_grad[0].T, rows)
    grad_part, came = lax.optimization_barrier((grad_part, came))
    grads = trade(grad_part, "depth")

    mine, sent = step(jnp.stack([kept, came]), far)
    came = swap(sent, "far")

    act_away, act_keep = act_call(val_lengths, mine, came, vals)
    halves = act_keep + swap(act_away, "core")
    act_mine = halves[:, 0] + swap(halves[:, 1], "pair")
    act_came = swap(act_mine, "far")

    terms = combine_call(spot, segment_ids, act_mine, act_came, grads)
    everyone = lax.axis_size(LAYERS)
    terms = trade(jnp.broadcast_to(terms[None], (everyone, 1, 128)), LAYERS).reshape(everyone, 128)
    norm = (tok_count * SLOTS * lax.axis_size("section")) ** -0.5
    return pl.pallas_call(
        functools.partial(total_kernel, norm),
        out_shape=jax.ShapeDtypeStruct((1, SEQ_DEV), jnp.float32),
        in_specs=[VMEM],
        out_specs=VMEM,
        compiler_params=params(),
    )(terms)


def solution(mesh):
    split = Mesh(mesh.devices.reshape(SHAPE), NAMES)
    placed = (
        P("section", PLANE, None),
        P("section", ("pair", "core"), TENSOR),
        P("section", PLANE, None),
        P("section", ("pair", "core"), TENSOR),
        P(("pair", "core"), None),
        P(),
    )
    return jax.shard_map(
        on_device, mesh=split, in_specs=placed, out_specs=P(("pair", "core"), None), check_vma=False
    )
```

```python
import functools
import jax
import jax.numpy as jnp
from jax import lax
from jax.experimental import pallas as pl
from jax.experimental.pallas import tpu as pltpu
from jax.sharding import Mesh, PartitionSpec as P

SEQ_DEV = 4
VSEQ = 8
VLEN = 64
SLOTS = VSEQ * VLEN
LIVE = 384
CODES = 32767.0

NAMES = ("section", "pair", "core", "far", "depth")
SHAPE = (8, 2, 2, 2, 8)
PLANE = ("pair", "core", "far", "depth")
SLICES = ("core", "pair", "far")
ACROSS = ("core", "pair", "far", "depth")
TENSOR = ("far", "depth")
LAYERS = ("section", "far", "depth")

SMEM = pl.BlockSpec(memory_space=pltpu.SMEM)
VMEM = pl.BlockSpec(memory_space=pltpu.VMEM)
LIMIT = 48 * 1024 * 1024


def swap(value, axis):
    return lax.ppermute(value, axis, [(0, 1), (1, 0)])


def swap_both(value):
    return lax.ppermute(value, ("pair", "far"), [(0, 3), (1, 2), (2, 1), (3, 0)])


def trade(value, axes):
    return lax.all_to_all(value, axes, 0, 0, tiled=True)


def dot(left, right, over):
    return lax.dot_general(left, right, (over, ((), ())), preferred_element_type=jnp.float32)


def params(**more):
    return pltpu.CompilerParams(vmem_limit_bytes=LIMIT, **more)


def cost(flops, moved):
    return pl.CostEstimate(flops=flops, bytes_accessed=moved, transcendentals=0)


def live_places(lens, seq, pos):
    place = jnp.full(seq.shape, -1, jnp.int32)
    start = jnp.int32(0)
    for number in range(VSEQ):
        count = lens[number]
        place = jnp.where((seq == number) & (pos < count), start + pos, place)
        start = start + count
    return place


def picker(place):
    wanted = lax.broadcasted_iota(jnp.int32, (LIVE, place.shape[1]), 0)
    return jnp.where(wanted == place, 1.0, 0.0).astype(jnp.bfloat16)


def spread_kernel(val, spread):
    count, _, piece = spread.shape
    parts = val.shape[1] // piece
    for part in range(parts):
        rows_here = val[:, part * piece : (part + 1) * piece]
        for turn in range(count // parts):
            spread[part * (count // parts) + turn] = rows_here


def spread_call(val, piece, count):
    return pl.pallas_call(
        spread_kernel,
        out_shape=jax.ShapeDtypeStruct((count, val.shape[0], piece), val.dtype),
        in_specs=[VMEM],
        out_specs=VMEM,
        compiler_params=params(),
        cost_estimate=cost(0, 2 * count * val.shape[0] * piece),
    )(val)


def beside_kernel(spot, own, train, beside):
    feats, rows = own.shape[0], train.shape[0]
    half = train.shape[1] // 2
    beside[0:feats, :] = own[...]
    for tile in range(half // 128):
        lanes = pl.ds(pl.multiple_of((1 - spot[1]) * half + tile * 128, 128), 128)
        beside[feats + tile * rows : feats + (tile + 1) * rows, :] = train[:, lanes]


def beside_call(spot, own, train):
    feats, lanes = own.shape
    extra = train.shape[0] * train.shape[1] // 2 // lanes
    return pl.pallas_call(
        beside_kernel,
        out_shape=jax.ShapeDtypeStruct((feats + extra, lanes), own.dtype),
        in_specs=[SMEM, VMEM, VMEM],
        out_specs=VMEM,
        compiler_params=params(),
        cost_estimate=cost(0, 4 * (own.size + train.size)),
    )(spot, own, train)


def slices_kernel(spot, train, got, own, to_pair, to_far, to_both):
    rows, piece = own.shape[1:]
    first = got.shape[0] - rows * (train.shape[1] // 2 // 128)
    per = piece // 128
    for flip, ref in enumerate((own, to_far, to_pair, to_both)):
        number = (spot[0] * 2 + spot[2]) ^ flip
        lanes = spot[1] * (train.shape[1] // 2) + number * piece
        ref[0] = train[:, pl.ds(pl.multiple_of(lanes, 128), piece)]
        for tile in range(per):
            at = pl.multiple_of(first + (number * per + tile) * rows, rows)
            ref[1, :, tile * 128 : (tile + 1) * 128] = got[pl.ds(at, rows), :]


def slices_call(spot, train, got, piece):
    shape = jax.ShapeDtypeStruct((2, train.shape[0], piece), train.dtype)
    return pl.pallas_call(
        slices_kernel,
        out_shape=(shape,) * 4,
        in_specs=[SMEM, VMEM, VMEM],
        out_specs=(VMEM,) * 4,
        compiler_params=params(),
        cost_estimate=cost(0, 8 * train.size),
    )(spot, train, got)


def live_part(spot, lens, left, right, first):
    here = spot[0] * 2 + spot[1]
    lane = lax.broadcasted_iota(jnp.int32, (1, SLOTS // 2), 1)
    quarter = SLOTS // 4
    owner = jnp.where(lane < quarter, here ^ first, here ^ (first + 1))
    within = lane % quarter
    place = live_places(lens, owner * 2 + within // VLEN, within % VLEN)
    return dot(picker(place), jnp.concatenate([left, right], axis=1), ((1,), (1,)))


def grad_kernel(spot, lens, own, beside, across, corner, train, out, scale):
    feats, toks = train.shape
    depth, _, rows, _ = out.shape
    near = live_part(spot, lens, own[...], beside[0:feats, :], 0)
    live = (near + live_part(spot, lens, across[...], corner[...], 2)).astype(jnp.bfloat16)
    for far in range(2):
        block = train[:, far * (toks // 2) : (far + 1) * (toks // 2)]
        gram = dot(live, block, ((1,), (0,))).T
        size = jnp.abs(gram)
        most = jnp.max(size)
        share = jnp.sqrt(size * jnp.where(most > 0.0, 1.0 / most, 0.0))
        code = jnp.round(jnp.where(gram < 0.0, -CODES, CODES) * share)
        out[:, far] = code.astype(jnp.int32).astype(jnp.int16).reshape(depth, rows, LIVE)
        scale[far * 8 : (far + 1) * 8, :] = jnp.full((8, 128), most, jnp.float32)


def grad_call(spot, lens, pieces, train, rows):
    feats, toks = train.shape
    return pl.pallas_call(
        grad_kernel,
        out_shape=(
            jax.ShapeDtypeStruct((toks // (2 * rows), 2, rows, LIVE), jnp.int16),
            jax.ShapeDtypeStruct((16, 128), jnp.float32),
        ),
        in_specs=[SMEM, SMEM] + [VMEM] * 5,
        out_specs=(VMEM, VMEM),
        compiler_params=params(),
        cost_estimate=cost(2 * toks * LIVE * feats, 2 * toks * feats + 4 * toks * LIVE),
    )(spot, lens, *pieces, train)


def act_kernel(lens, own, pair, far, both, vals, away, keep):
    slots = vals.shape[0]
    lane = lax.broadcasted_iota(jnp.int32, (1, slots), 1)
    block = lane // VLEN
    seq = (block // 2 % 2) * 4 + (block // 4) * 2 + block % 2
    chosen = picker(live_places(lens, seq, lane % VLEN))
    live = dot(chosen, vals[...], ((1,), (0,))).astype(jnp.bfloat16)
    for flip, ref in enumerate((keep, away)):
        left = jnp.concatenate([part[flip] for part in (own, pair, far, both)], axis=0)
        ref[...] = dot(left, live, ((1,), (1,))).reshape(ref.shape)


def act_call(lens, own, pair, far, both, vals):
    rows, piece = own.shape[1:]
    shape = jax.ShapeDtypeStruct((2, 2, rows, LIVE), jnp.float32)
    count = 8 * rows
    return pl.pallas_call(
        act_kernel,
        out_shape=(shape, shape),
        in_specs=[SMEM] + [VMEM] * 5,
        out_specs=(VMEM, VMEM),
        compiler_params=params(),
        cost_estimate=cost(2 * (count + SLOTS) * LIVE * piece, 4 * SLOTS * piece + 4 * count * LIVE),
    )(lens, own, pair, far, both, vals)


def combine_kernel(spot, ids, own, pair, away, both, grads, scale, out):
    depth, _, rows, _ = grads.shape
    per = 128 // rows
    row = lax.broadcasted_iota(jnp.int32, (8, 128), 0)
    lane = lax.broadcasted_iota(jnp.int32, (8, 128), 1)
    seqs = lax.broadcasted_iota(jnp.int32, (8, rows), 0)
    sums = jnp.zeros((8, 128), jnp.float32)
    for far in range(2):
        number = far * depth + spot[3]
        lanes = ids[:, pl.ds(pl.multiple_of((number // per) * 128, 128), 128)]
        owner = lanes[:, :rows]
        for turn in range(1, per):
            owner = jnp.where(number % per == turn, lanes[:, turn * rows : (turn + 1) * rows], owner)
        flip = spot[2] ^ far
        act = own[flip] + pair[flip] + away[1 - flip] + both[1 - flip]
        folded = []
        for other in range(depth):
            code = grads[other, far].astype(jnp.int32).astype(jnp.float32)
            terms = act * (code * jnp.abs(code))
            folded.append(sum(terms[:, at : at + 128] for at in range(0, LIVE, 128)))
        held = lax.dot_general(
            jnp.where(seqs == owner, 1.0, 0.0), jnp.concatenate(folded, axis=1), (((1,), (0,)), ((), ())),
            precision=lax.Precision.HIGHEST, preferred_element_type=jnp.float32,
        )
        for other in range(depth):
            column = jnp.sum(held[:, other * 128 : (other + 1) * 128], axis=1, keepdims=True)
            sums = jnp.where(lane // SEQ_DEV == far * depth + other, column, sums)
    place = lane % 64
    value = jnp.where((row == lane % SEQ_DEV) & (lane < 64), sums, 0.0)
    block = jnp.where(place // (SEQ_DEV * depth) == 0, scale[0:8], scale[8:16])
    mine = (row == 0) & (lane >= 64) & (place // SEQ_DEV % depth == spot[3])
    out[...] = jnp.sum(jnp.where(mine, block, value), axis=0, keepdims=True)


def combine_call(spot, ids, acts, grads, scale):
    return pl.pallas_call(
        combine_kernel,
        out_shape=jax.ShapeDtypeStruct((1, 128), jnp.float32),
        in_specs=[SMEM] + [VMEM] * 7,
        out_specs=VMEM,
        compiler_params=params(),
        cost_estimate=cost(4 * grads.size, 4 * grads.size),
    )(spot, ids, *acts, grads, scale)


def total_kernel(depth, norm, terms, out):
    count = terms.shape[0]
    groups = jnp.sum(terms[...].reshape(count // depth, depth, 128), axis=1)
    lane = lax.broadcasted_iota(jnp.int32, groups.shape, 1)
    scaled = jnp.where(lane < 64, groups * pltpu.roll(groups, 64, 1), 0.0)
    whole = jnp.sum(scaled, axis=0, keepdims=True)
    lane = lax.broadcasted_iota(jnp.int32, whole.shape, 1)
    scores = [
        jnp.sum(jnp.where(lane % SEQ_DEV == seq, whole, 0.0), axis=1, keepdims=True) for seq in range(SEQ_DEV)
    ]
    out[...] = jnp.concatenate(scores, axis=1) * (norm / (CODES * CODES))


def on_device(train_act, train_grad, val_act, val_grad, segment_ids, val_lengths):
    tok_count = segment_ids.shape[1]
    rows, width = train_act.shape[1:]
    val_rows = val_act.shape[1]
    parts = lax.axis_size(SLICES)
    depth = lax.axis_size("depth")
    piece = width // parts
    pair, core, far, deep = (lax.axis_index(name) for name in PLANE)
    spot = jnp.stack([pair, core, far, deep]).astype(jnp.int32)

    own = val_grad[0].T
    across = swap(own, "pair")
    later, across = lax.optimization_barrier((spot, across))
    corner = swap(across, "core")
    beside = swap(beside_call(later, own, train_act[0]), "core")

    vals = trade(spread_call(val_act[0], piece, parts * depth), ACROSS).reshape(SLOTS, piece)
    mine, to_pair, to_far, to_both = slices_call(spot, train_act[0], beside, piece)
    parts_in = (mine, swap(to_pair, "pair"), swap(to_far, "far"), swap_both(to_both))

    grad_part, scale = grad_call(spot, val_lengths, (own, beside, across, corner), train_grad[0].T, rows)
    grad_part, *parts_in = lax.optimization_barrier((grad_part, *parts_in))
    grads = trade(grad_part, "depth")

    act_away, act_keep = act_call(val_lengths, *parts_in, vals)
    halves = act_keep + swap(act_away, "core")
    mine, other = halves[:, 0], halves[:, 1]
    acts = (mine, swap(other, "pair"), swap(mine, "far"), swap_both(other))

    terms = combine_call(spot, segment_ids, acts, grads, scale)
    everyone = lax.axis_size(LAYERS)
    terms = trade(jnp.broadcast_to(terms[None], (everyone, 1, 128)), LAYERS).reshape(everyone, 128)
    norm = (tok_count * SLOTS * lax.axis_size("section")) ** -0.5
    return pl.pallas_call(
        functools.partial(total_kernel, depth, norm),
        out_shape=jax.ShapeDtypeStruct((1, SEQ_DEV), jnp.float32),
        in_specs=[VMEM],
        out_specs=VMEM,
        compiler_params=params(),
    )(terms)


def solution(mesh):
    split = Mesh(mesh.devices.reshape(SHAPE), NAMES)
    placed = (
        P("section", PLANE, None),
        P("section", ("pair", "core"), TENSOR),
        P("section", PLANE, None),
        P("section", ("pair", "core"), TENSOR),
        P(("pair", "core"), None),
        P(),
    )
    return jax.shard_map(
        on_device, mesh=split, in_specs=placed, out_specs=P(("pair", "core"), None), check_vma=False
    )
```

```python
import functools
import jax
import jax.numpy as jnp
from jax import lax
from jax.experimental import pallas as pl
from jax.experimental.pallas import tpu as pltpu
from jax.sharding import Mesh, PartitionSpec as P

SEQ_DEV = 4
VSEQ = 8
VLEN = 64
SLOTS = VSEQ * VLEN
LIVE = 384
CODES = 32767.0

NAMES = ("section", "pair", "core", "far", "depth")
SHAPE = (8, 2, 2, 2, 8)
PLANE = ("pair", "core", "far", "depth")
SLICES = ("core", "pair", "far")
ACROSS = ("core", "pair", "far", "depth")
TENSOR = ("far", "depth")
LAYERS = ("section", "far", "depth")

SMEM = pl.BlockSpec(memory_space=pltpu.SMEM)
VMEM = pl.BlockSpec(memory_space=pltpu.VMEM)
LIMIT = 48 * 1024 * 1024


def swap(value, axis):
    return lax.ppermute(value, axis, [(0, 1), (1, 0)])


def swap_both(value):
    return lax.ppermute(value, ("pair", "far"), [(0, 3), (1, 2), (2, 1), (3, 0)])


def trade(value, axes):
    return lax.all_to_all(value, axes, 0, 0, tiled=True)


def dot(left, right, over):
    return lax.dot_general(left, right, (over, ((), ())), preferred_element_type=jnp.float32)


def params(**more):
    return pltpu.CompilerParams(vmem_limit_bytes=LIMIT, **more)


def cost(flops, moved):
    return pl.CostEstimate(flops=flops, bytes_accessed=moved, transcendentals=0)


def live_places(lens, seq, pos):
    place = jnp.full(seq.shape, -1, jnp.int32)
    start = jnp.int32(0)
    for number in range(VSEQ):
        count = lens[number]
        place = jnp.where((seq == number) & (pos < count), start + pos, place)
        start = start + count
    return place


def picker(place):
    wanted = lax.broadcasted_iota(jnp.int32, (LIVE, place.shape[1]), 0)
    return jnp.where(wanted == place, 1.0, 0.0).astype(jnp.bfloat16)


def spread_kernel(val, spread):
    count, _, piece = spread.shape
    parts = val.shape[1] // piece
    for part in range(parts):
        rows_here = val[:, part * piece : (part + 1) * piece]
        for turn in range(count // parts):
            spread[part * (count // parts) + turn] = rows_here


def spread_call(val, piece, count):
    return pl.pallas_call(
        spread_kernel,
        out_shape=jax.ShapeDtypeStruct((count, val.shape[0], piece), val.dtype),
        in_specs=[VMEM],
        out_specs=VMEM,
        compiler_params=params(),
        cost_estimate=cost(4_000_000_000, 2 * count * val.shape[0] * piece),
    )(val)


def beside_kernel(spot, own, train, beside):
    feats, rows = own.shape[0], train.shape[0]
    half = train.shape[1] // 2
    beside[0:feats, :] = own[...]
    for tile in range(half // 128):
        lanes = pl.ds(pl.multiple_of((1 - spot[1]) * half + tile * 128, 128), 128)
        beside[feats + tile * rows : feats + (tile + 1) * rows, :] = train[:, lanes]


def beside_call(spot, own, train):
    feats, lanes = own.shape
    extra = train.shape[0] * train.shape[1] // 2 // lanes
    return pl.pallas_call(
        beside_kernel,
        out_shape=jax.ShapeDtypeStruct((feats + extra, lanes), own.dtype),
        in_specs=[SMEM, VMEM, VMEM],
        out_specs=VMEM,
        compiler_params=params(),
        cost_estimate=cost(0, 4 * (own.size + train.size)),
    )(spot, own, train)


def slices_kernel(spot, train, got, own, to_pair, to_far, to_both):
    rows, piece = own.shape[1:]
    first = got.shape[0] - rows * (train.shape[1] // 2 // 128)
    per = piece // 128
    for flip, ref in enumerate((own, to_far, to_pair, to_both)):
        number = (spot[0] * 2 + spot[2]) ^ flip
        lanes = spot[1] * (train.shape[1] // 2) + number * piece
        ref[0] = train[:, pl.ds(pl.multiple_of(lanes, 128), piece)]
        for tile in range(per):
            at = pl.multiple_of(first + (number * per + tile) * rows, rows)
            ref[1, :, tile * 128 : (tile + 1) * 128] = got[pl.ds(at, rows), :]


def slices_call(spot, train, got, piece):
    shape = jax.ShapeDtypeStruct((2, train.shape[0], piece), train.dtype)
    return pl.pallas_call(
        slices_kernel,
        out_shape=(shape,) * 4,
        in_specs=[SMEM, VMEM, VMEM],
        out_specs=(VMEM,) * 4,
        compiler_params=params(),
        cost_estimate=cost(0, 8 * train.size),
    )(spot, train, got)


def live_part(spot, lens, left, right, first):
    here = spot[0] * 2 + spot[1]
    lane = lax.broadcasted_iota(jnp.int32, (1, SLOTS // 2), 1)
    quarter = SLOTS // 4
    owner = jnp.where(lane < quarter, here ^ first, here ^ (first + 1))
    within = lane % quarter
    place = live_places(lens, owner * 2 + within // VLEN, within % VLEN)
    return dot(picker(place), jnp.concatenate([left, right], axis=1), ((1,), (1,)))


def grad_kernel(spot, lens, own, beside, across, corner, train, out, scale):
    feats, toks = train.shape
    depth, _, rows, _ = out.shape
    near = live_part(spot, lens, own[...], beside[0:feats, :], 0)
    live = (near + live_part(spot, lens, across[...], corner[...], 2)).astype(jnp.bfloat16)
    for far in range(2):
        block = train[:, far * (toks // 2) : (far + 1) * (toks // 2)]
        gram = dot(live, block, ((1,), (0,))).T
        size = jnp.abs(gram)
        most = jnp.max(size)
        share = jnp.sqrt(size * jnp.where(most > 0.0, 1.0 / most, 0.0))
        code = jnp.round(jnp.where(gram < 0.0, -CODES, CODES) * share)
        out[:, far] = code.astype(jnp.int32).astype(jnp.int16).reshape(depth, rows, LIVE)
        scale[far * 8 : (far + 1) * 8, :] = jnp.full((8, 128), most, jnp.float32)


def grad_call(spot, lens, pieces, train, rows):
    feats, toks = train.shape
    return pl.pallas_call(
        grad_kernel,
        out_shape=(
            jax.ShapeDtypeStruct((toks // (2 * rows), 2, rows, LIVE), jnp.int16),
            jax.ShapeDtypeStruct((16, 128), jnp.float32),
        ),
        in_specs=[SMEM, SMEM] + [VMEM] * 5,
        out_specs=(VMEM, VMEM),
        compiler_params=params(),
        cost_estimate=cost(2 * toks * LIVE * feats, 2 * toks * feats + 4 * toks * LIVE),
    )(spot, lens, *pieces, train)


def act_kernel(lens, own, pair, far, both, vals, away, keep):
    slots = vals.shape[0]
    lane = lax.broadcasted_iota(jnp.int32, (1, slots), 1)
    block = lane // VLEN
    seq = (block // 2 % 2) * 4 + (block // 4) * 2 + block % 2
    chosen = picker(live_places(lens, seq, lane % VLEN))
    live = dot(chosen, vals[...], ((1,), (0,))).astype(jnp.bfloat16)
    for flip, ref in enumerate((keep, away)):
        left = jnp.concatenate([part[flip] for part in (own, pair, far, both)], axis=0)
        ref[...] = dot(left, live, ((1,), (1,))).reshape(ref.shape)


def act_call(lens, own, pair, far, both, vals):
    rows, piece = own.shape[1:]
    shape = jax.ShapeDtypeStruct((2, 2, rows, LIVE), jnp.float32)
    count = 8 * rows
    return pl.pallas_call(
        act_kernel,
        out_shape=(shape, shape),
        in_specs=[SMEM] + [VMEM] * 5,
        out_specs=(VMEM, VMEM),
        compiler_params=params(),
        cost_estimate=cost(2 * (count + SLOTS) * LIVE * piece, 4 * SLOTS * piece + 4 * count * LIVE),
    )(lens, own, pair, far, both, vals)


def combine_kernel(spot, ids, own, pair, away, both, grads, scale, out):
    depth, _, rows, _ = grads.shape
    per = 128 // rows
    row = lax.broadcasted_iota(jnp.int32, (8, 128), 0)
    lane = lax.broadcasted_iota(jnp.int32, (8, 128), 1)
    seqs = lax.broadcasted_iota(jnp.int32, (8, rows), 0)
    sums = jnp.zeros((8, 128), jnp.float32)
    for far in range(2):
        number = far * depth + spot[3]
        lanes = ids[:, pl.ds(pl.multiple_of((number // per) * 128, 128), 128)]
        owner = lanes[:, :rows]
        for turn in range(1, per):
            owner = jnp.where(number % per == turn, lanes[:, turn * rows : (turn + 1) * rows], owner)
        flip = spot[2] ^ far
        act = own[flip] + pair[flip] + away[1 - flip] + both[1 - flip]
        folded = []
        for other in range(depth):
            code = grads[other, far].astype(jnp.int32).astype(jnp.float32)
            terms = act * (code * jnp.abs(code))
            folded.append(sum(terms[:, at : at + 128] for at in range(0, LIVE, 128)))
        held = lax.dot_general(
            jnp.where(seqs == owner, 1.0, 0.0), jnp.concatenate(folded, axis=1), (((1,), (0,)), ((), ())),
            precision=lax.Precision.HIGHEST, preferred_element_type=jnp.float32,
        )
        for other in range(depth):
            column = jnp.sum(held[:, other * 128 : (other + 1) * 128], axis=1, keepdims=True)
            sums = jnp.where(lane // SEQ_DEV == far * depth + other, column, sums)
    place = lane % 64
    value = jnp.where((row == lane % SEQ_DEV) & (lane < 64), sums, 0.0)
    block = jnp.where(place // (SEQ_DEV * depth) == 0, scale[0:8], scale[8:16])
    mine = (row == 0) & (lane >= 64) & (place // SEQ_DEV % depth == spot[3])
    out[...] = jnp.sum(jnp.where(mine, block, value), axis=0, keepdims=True)


def combine_call(spot, ids, acts, grads, scale):
    return pl.pallas_call(
        combine_kernel,
        out_shape=jax.ShapeDtypeStruct((1, 128), jnp.float32),
        in_specs=[SMEM] + [VMEM] * 7,
        out_specs=VMEM,
        compiler_params=params(),
        cost_estimate=cost(4 * grads.size, 4 * grads.size),
    )(spot, ids, *acts, grads, scale)


def total_kernel(depth, norm, terms, out):
    count = terms.shape[0]
    groups = jnp.sum(terms[...].reshape(count // depth, depth, 128), axis=1)
    lane = lax.broadcasted_iota(jnp.int32, groups.shape, 1)
    scaled = jnp.where(lane < 64, groups * pltpu.roll(groups, 64, 1), 0.0)
    whole = jnp.sum(scaled, axis=0, keepdims=True)
    lane = lax.broadcasted_iota(jnp.int32, whole.shape, 1)
    scores = [
        jnp.sum(jnp.where(lane % SEQ_DEV == seq, whole, 0.0), axis=1, keepdims=True) for seq in range(SEQ_DEV)
    ]
    out[...] = jnp.concatenate(scores, axis=1) * (norm / (CODES * CODES))


def on_device(train_act, train_grad, val_act, val_grad, segment_ids, val_lengths):
    tok_count = segment_ids.shape[1]
    rows, width = train_act.shape[1:]
    val_rows = val_act.shape[1]
    parts = lax.axis_size(SLICES)
    depth = lax.axis_size("depth")
    piece = width // parts
    pair, core, far, deep = (lax.axis_index(name) for name in PLANE)
    spot = jnp.stack([pair, core, far, deep]).astype(jnp.int32)

    own = val_grad[0].T
    across = swap(own, "pair")
    beside = beside_call(spot, own, train_act[0])
    beside, across = lax.optimization_barrier((beside, across))
    corner = swap(across, "core")
    beside = swap(beside, "core")

    vals = trade(spread_call(val_act[0], piece, parts * depth), ACROSS).reshape(SLOTS, piece)
    mine, to_pair, to_far, to_both = slices_call(spot, train_act[0], beside, piece)
    parts_in = (mine, swap(to_pair, "pair"), swap(to_far, "far"), swap_both(to_both))

    grad_part, scale = grad_call(spot, val_lengths, (own, beside, across, corner), train_grad[0].T, rows)
    grad_part, *parts_in = lax.optimization_barrier((grad_part, *parts_in))
    act_away, act_keep = act_call(val_lengths, *parts_in, vals)
    grad_part, act_away = lax.optimization_barrier((grad_part, act_away))
    grads = trade(grad_part, "depth")
    halves = act_keep + swap(act_away, "core")
    mine, other = halves[:, 0], halves[:, 1]
    acts = (mine, swap(other, "pair"), swap(mine, "far"), swap_both(other))

    terms = combine_call(spot, segment_ids, acts, grads, scale)
    everyone = lax.axis_size(LAYERS)
    terms = trade(jnp.broadcast_to(terms[None], (everyone, 1, 128)), LAYERS).reshape(everyone, 128)
    norm = (tok_count * SLOTS * lax.axis_size("section")) ** -0.5
    return pl.pallas_call(
        functools.partial(total_kernel, depth, norm),
        out_shape=jax.ShapeDtypeStruct((1, SEQ_DEV), jnp.float32),
        in_specs=[VMEM],
        out_specs=VMEM,
        compiler_params=params(),
    )(terms)


def solution(mesh):
    split = Mesh(mesh.devices.reshape(SHAPE), NAMES)
    placed = (
        P("section", PLANE, None),
        P("section", ("pair", "core"), TENSOR),
        P("section", PLANE, None),
        P("section", ("pair", "core"), TENSOR),
        P(("pair", "core"), None),
        P(),
    )
    return jax.shard_map(
        on_device, mesh=split, in_specs=placed, out_specs=P(("pair", "core"), None), check_vma=False
    )
```
